32 devices in a mesh: real: 2 (over x), up: 8 (over z, y), dn: 2 (over core).
Axes of the slice: x: 2, y: 2, z: 4, core: 2. Of those that a mesh axis runs over, the one named last changes fastest.
Arguments:
- start: float32 [6, 2048, 2048], P('real', 'up', 'dn'), parts along dimension 0, may hold values from -700 to 700
- up_occupied: int32 [2048, 14], P('up'), may hold values 0 or 1
- dn_occupied: int32 [2048, 14], P('dn'), may hold values 0 or 1
- disorder: float32 [28], P('real'), parts along dimension 0, may hold values from -1.5 to 1.5
- hop_tiles: float32 [16, 128, 128], replicated, may hold values from -0.15625 to 0.15625
- up_index: int32 [16, 5], replicated, may hold values from 0 to 15
- dn_index: int32 [16, 5], replicated, may hold values from 0 to 15
Outputs:
- filtered: float32 [6, 2048, 2048], P('real', 'up', 'dn'), parts along dimension 0
- gram: float32 [4, 3, 3], P('real'), parts along dimension 0
The draws below stay inside these ranges and needn't reach their ends.
There are 2 independent parts, one for each index of `real`. The reference program is written for one: setup_inputs(seed, part) draws one part's arguments, and reference() takes and returns one part's arrays. A program takes and returns all parts, laid end to end along the dimension named above; an argument that names none is the same for every part. Nothing has to cross between parts.
All inputs are finite; a program needn't handle non-finite values. No bound on the sum of `up_occupied` or of `dn_occupied` on one device may be relied on, other than what follows from the above.
Results may differ from the reference program's by a relative error of at most 0.0001.
Values sent between devices are 32-bit elements; how exact they have to be, the bound alone decides.
A program may use at most 192 MiB of HBM per device.

```python
import jax
import jax.numpy as jnp
import numpy as np
from jax import lax

L = 14
TILE = 128
NV = 3
NTILE = 16
UBITS = 4
DBITS = 4
NBU = 16
NBD = 16
NU = 2048
ND = 2048


def draw_start(key, part):
    key = jax.random.fold_in(key, 11)
    first_key, second_key = jax.random.split(key, 2)
    place = jnp.arange(NU, dtype=jnp.float32) / NU
    column_scale = jnp.exp(2.3 * jax.random.uniform(second_key, (ND,), jnp.float32))
    values = jnp.clip(jax.random.normal(first_key, (NV, NU, ND), jnp.float32), -6.0, 6.0)
    row_scale = jnp.exp(2.3 * place)
    return values * row_scale[None, :, None] * column_scale[None, None, :]


def plant(values, stream_key, low, high):
    longest = values.shape.index(max(values.shape))
    spots = []
    for shift in (0, 1):
        where = [jax.random.randint(jax.random.fold_in(stream_key, axis), (), 0, length) for axis, length in enumerate(values.shape)]
        where[longest] = (where[longest] + shift) % values.shape[longest]
        spots.append(tuple(where))
    return values.at[spots[0]].set(low).at[spots[1]].set(high)


def normal_values(stream_key, dims, scale, bound, kind=jnp.bfloat16):
    values = jax.random.normal(stream_key, dims, jnp.float32) * scale
    return jnp.minimum(jnp.maximum(values, -bound), bound).astype(kind)


def setup_inputs(seed: int = 0, part: int = 0) -> dict:
    key_of = jax.random.split(jax.random.key(seed), 8)
    own_keys = jax.random.split(jax.random.fold_in(key_of[7], part), 8)
    return {
        "start": draw_start(jax.random.fold_in(jax.random.fold_in(key_of[7], part), 71), part),
        "up_occupied": plant((jax.random.randint(key_of[1], (NU, L), 0, 2) < 1).astype(jnp.int32), jax.random.fold_in(key_of[1], 1), 0, 1),
        "dn_occupied": plant((jax.random.randint(key_of[2], (ND, L), 0, 2) < 1).astype(jnp.int32), jax.random.fold_in(key_of[2], 1), 0, 1),
        "disorder": jnp.clip(jax.random.uniform(own_keys[3], (L,), jnp.float32, -1.5, 1.5), -1.5, 1.5),
        "hop_tiles": normal_values(key_of[4], (NTILE, TILE, TILE), (TILE * (UBITS + DBITS + 2)) ** -0.5, 0.15625, jnp.float32),
        "up_index": plant(jax.random.randint(key_of[5], (NBU, UBITS + 1), 0, NTILE), jax.random.fold_in(key_of[5], 1), 0, NTILE - 1).astype(jnp.int32),
        "dn_index": plant(jax.random.randint(key_of[6], (NBD, DBITS + 1), 0, NTILE), jax.random.fold_in(key_of[6], 1), 0, NTILE - 1).astype(jnp.int32),
    }


highest = lax.Precision.HIGHEST

def pair_tiles(bank, table, rows, bit):
    others = rows ^ 1 << bit
    lower = jnp.minimum(rows, others)
    picked = bank[table[lower, bit + 1]]
    flipped = jnp.swapaxes(picked, 1, 2)
    return jnp.where((rows < others)[:, None, None], picked, flipped)

def own_tiles(bank, table, rows):
    picked = bank[table[rows, 0]]
    return 0.5 * (picked + jnp.swapaxes(picked, 1, 2))

def row_terms(blocks, rows, bank, table, local_bits):
    total = jnp.einsum('jab,vjbc->vjac', own_tiles(bank, table, rows), blocks, precision=highest)
    for bit in range(local_bits):
        partner = np.arange(blocks.shape[1]) ^ 1 << bit
        total = total + jnp.einsum('jab,vjbc->vjac', pair_tiles(bank, table, rows, bit), blocks[:, partner], precision=highest)
    return total

def column_terms(blocks, rows, bank, table, local_bits):
    total = jnp.einsum('jab,vujb->vuja', own_tiles(bank, table, rows), blocks, precision=highest)
    for bit in range(local_bits):
        partner = np.arange(blocks.shape[2]) ^ 1 << bit
        total = total + jnp.einsum('jab,vujb->vuja', pair_tiles(bank, table, rows, bit), blocks[:, :, partner], precision=highest)
    return total

def operate(field, potential, bank, up_table, dn_table, shift):
    width = bank.shape[1]
    up_count = field.shape[1] // width
    dn_count = field.shape[2] // width
    up_rows = jnp.arange(up_count, dtype=jnp.int32)
    dn_rows = jnp.arange(dn_count, dtype=jnp.int32)
    up_blocks = field.reshape(field.shape[0], up_count, width, field.shape[2])
    dn_blocks = field.reshape(field.shape[0], field.shape[1], dn_count, width)
    up_part = row_terms(up_blocks, up_rows, bank, up_table, up_count.bit_length() - 1).reshape(field.shape)
    dn_part = column_terms(dn_blocks, dn_rows, bank, dn_table, dn_count.bit_length() - 1).reshape(field.shape)
    return up_part + dn_part + (potential - shift)[None] * field

def reference(start, up_occupied, dn_occupied, disorder, hop_tiles, up_index, dn_index):
    up_float = up_occupied.astype(jnp.float32)
    dn_float = dn_occupied.astype(jnp.float32)
    potential = jnp.dot(up_float, dn_float.T, precision=highest)
    potential = potential + jnp.dot(up_float, disorder, precision=highest)[:, None]
    potential = potential + jnp.dot(dn_float, disorder, precision=highest)[None, :]
    shift = 0.25 * L
    cells = NU * ND
    first = operate(start, potential, hop_tiles, up_index, dn_index, shift)
    scale = jnp.sqrt(lax.optimization_barrier(jnp.sum(first * first, axis=(1, 2))) / cells + 1e-06)
    normed = first / scale[:, None, None]
    filtered = operate(normed, potential, hop_tiles, up_index, dn_index, shift)
    correlation = jnp.einsum('vud,wud->vw', normed, normed, precision=highest)
    image = jnp.einsum('vud,wud->vw', normed, filtered, precision=highest)
    gram = jnp.stack([correlation, image]) / cells
    return (filtered, gram)
```

```python
import jax
import jax.numpy as jnp
import numpy as np
from jax import lax
from jax.experimental import pallas as pl
from jax.experimental.pallas import tpu as pltpu
from jax.sharding import PartitionSpec as P

highest = lax.Precision.HIGHEST


def swapped(block, axis, bit):
    count = lax.axis_size(axis)
    route = []
    for low in range(count):
        high = low | 1 << bit
        if high != low and high < count:
            route += [(low, high), (high, low)]
    return lax.ppermute(block, axis, route)


def pair_tiles(bank, table, rows, bit):
    others = rows ^ 1 << bit
    lower = jnp.minimum(rows, others)
    picked = bank[table[lower, bit + 1]]
    flipped = jnp.swapaxes(picked, 1, 2)
    return jnp.where((rows < others)[:, None, None], picked, flipped)


def own_tiles(bank, table, rows):
    picked = bank[table[rows, 0]]
    return 0.5 * (picked + jnp.swapaxes(picked, 1, 2))


def row_terms(blocks, rows, bank, table):
    total = jnp.einsum("jab,vjbc->vjac", own_tiles(bank, table, rows), blocks, precision=highest)
    partner = np.arange(blocks.shape[1]) ^ 1 << 0
    total = total + jnp.einsum(
        "jab,vjbc->vjac", pair_tiles(bank, table, rows, 0), blocks[:, partner], precision=highest
    )
    return total


def column_terms(blocks, rows, bank, table, local_bits):
    total = jnp.einsum("jab,vujb->vuja", own_tiles(bank, table, rows), blocks, precision=highest)
    for bit in range(local_bits):
        partner = np.arange(blocks.shape[2]) ^ 1 << bit
        total = total + jnp.einsum(
            "jab,vujb->vuja",
            pair_tiles(bank, table, rows, bit),
            blocks[:, :, partner],
            precision=highest,
        )
    return total


def up_swapped(field, bank, table):
    width = bank.shape[1]
    local = field.shape[1] // width
    local_bits = local.bit_length() - 1
    rows = lax.axis_index("up") * local + jnp.arange(local, dtype=jnp.int32)
    shape = (field.shape[0], local, width, field.shape[2])
    total = row_terms(field.reshape(shape), rows, bank, table)
    for level in range(lax.axis_size("up").bit_length() - 1):
        other = swapped(field, "up", level)
        tiles = pair_tiles(bank, table, rows, local_bits + level)
        total = total + jnp.einsum("jab,vjbc->vjac", tiles, other.reshape(shape), precision=highest)
    return total.reshape(field.shape)


def dn_swapped(field, bank, table):
    width = bank.shape[1]
    local = field.shape[2] // width
    local_bits = local.bit_length() - 1
    rows = lax.axis_index("dn") * local + jnp.arange(local, dtype=jnp.int32)
    shape = (field.shape[0], field.shape[1], local, width)
    total = column_terms(field.reshape(shape), rows, bank, table, local_bits)
    other = swapped(field, "dn", 0)
    tiles = pair_tiles(bank, table, rows, local_bits)
    total = total + jnp.einsum("jab,vujb->vuja", tiles, other.reshape(shape), precision=highest)
    return total.reshape(field.shape)


def operate(field, potential, bank, up_table, dn_table, shift):
    up_part = up_swapped(field, bank, up_table)
    dn_part = dn_swapped(field, bank, dn_table)
    return up_part + dn_part + (potential - shift)[None] * field


def body(start, up_occupied, dn_occupied, disorder, hop_tiles, up_index, dn_index):
    up_float = up_occupied.astype(jnp.float32)
    dn_float = dn_occupied.astype(jnp.float32)
    potential = jnp.dot(up_float, dn_float.T, precision=highest)
    potential = potential + jnp.dot(up_float, disorder, precision=highest)[:, None]
    potential = potential + jnp.dot(dn_float, disorder, precision=highest)[None, :]
    shift = 0.25 * up_occupied.shape[1]
    cells = start.shape[1] * start.shape[2] * lax.axis_size("up") * lax.axis_size("dn")
    first = operate(start, potential, hop_tiles, up_index, dn_index, shift)
    second = operate(first, potential, hop_tiles, up_index, dn_index, shift)
    correlation, image = lax.psum(
        (
            jnp.einsum("vud,wud->vw", first, first, precision=highest),
            jnp.einsum("vud,wud->vw", first, second, precision=highest),
        ),
        ("up", "dn"),
    )
    scale = jnp.sqrt(jnp.diagonal(correlation) / cells + 1e-06)
    outer = scale[:, None] * scale[None, :]
    gram = jnp.stack([correlation / outer, image / outer]) / cells
    return (second / scale[:, None, None], gram)


MESH = pl.DeviceIdType.MESH
HALF = 512
ROWS = 256
PAIRS = [(0, 0), (0, 1), (0, 2), (1, 1), (1, 2), (2, 2)]


def split(value):
    high = value.astype(jnp.bfloat16)
    return high, (value - high.astype(jnp.float32)).astype(jnp.bfloat16)


def product(a, b):
    def dot(p, q):
        return jnp.dot(p, q, preferred_element_type=jnp.float32)

    return dot(a[0], b[0]) + (dot(a[1], b[0]) + dot(a[0], b[1]))


def kernel(
    x_ref, pay_ref, dn_ref, bank_ref, uidx_ref, didx_ref,
    out_ref, stat_ref,
    field, got, side, pot, xh, xl, uh, ul, dh, dl, urh, url, drh, drl,
    rsend, rrecv, osend, orecv, bsend, brecv, psend, precv,
):
    x, up, core = lax.axis_index("real"), lax.axis_index("up"), lax.axis_index("dn")
    z, y = up // 2, up % 2
    h, low = z // 2, z % 2

    def device(px, ph, plow=low, py=y, pc=core):
        return (px, (ph * 2 + plow) * 2 + py, pc)

    partners = [
        device(x, h, pc=1 - core),
        device(1 - x, h),
        device(x, h, py=1 - y),
        device(x, h, plow=1 - low),
    ]
    barrier = pltpu.get_barrier_semaphore()
    for partner in partners + [device(x, 1 - h), device(1 - x, 1 - h)]:
        pl.semaphore_signal(barrier, inc=1, device_id=partner, device_id_type=MESH)
    pl.semaphore_wait(barrier, 6)

    def remote(src, dst, send, recv, target):
        return pltpu.make_async_remote_copy(
            src_ref=src, dst_ref=dst, send_sem=send, recv_sem=recv,
            device_id=target, device_id_type=MESH,
        )

    on_diagonal = x == h

    def regroup(v):
        rows = pl.ds(pl.multiple_of(h * ROWS, ROWS), ROWS)
        near = x_ref.at[v, :, pl.ds(pl.multiple_of(h * HALF, HALF), HALF)]
        far = x_ref.at[v, :, pl.ds(pl.multiple_of((1 - h) * HALF, HALF), HALF)]
        dst = field.at[v, rows, :]
        return (
            pltpu.make_async_copy(near, dst, rrecv.at[v, 0]),
            remote(near, dst, rsend.at[v, 0], rrecv.at[v, 0], device(h, x)),
            remote(far, dst, rsend.at[v, 1], rrecv.at[v, 1], device(1 - h, x)),
        )

    def restore(v):
        near = field.at[6 + v, pl.ds(pl.multiple_of(x * ROWS, ROWS), ROWS), :]
        far = field.at[6 + v, pl.ds(pl.multiple_of((1 - x) * ROWS, ROWS), ROWS), :]
        dst = out_ref.at[v, :, pl.ds(pl.multiple_of(x * HALF, HALF), HALF)]
        return (
            pltpu.make_async_copy(near, dst, brecv.at[v, 0]),
            remote(near, dst, bsend.at[v, 0], brecv.at[v, 0], device(h, x)),
            remote(far, dst, bsend.at[v, 1], brecv.at[v, 1], device(h, 1 - x)),
        )

    def start(copies):
        own, near, far = copies

        @pl.when(on_diagonal)
        def _():
            own.start()

        @pl.when(jnp.logical_not(on_diagonal))
        def _():
            near.start()

        far.start()

    def finish(copies):
        own, near, far = copies

        @pl.when(on_diagonal)
        def _():
            own.wait()

        @pl.when(jnp.logical_not(on_diagonal))
        def _():
            near.wait()

        far.wait()

    def exchange(t, d):
        return remote(field.at[t], got.at[t, d], osend.at[t, d], orecv.at[t, d], partners[d])

    side_copies = [
        remote(pay_ref, side.at[0], psend.at[0], precv.at[0], device(x, 1 - h)),
        remote(pay_ref, side.at[1], psend.at[1], precv.at[1], device(1 - x, h)),
    ]
    start(regroup(0))
    for copy in side_copies:
        copy.start()


    def pair(table, r, k):
        p = r ^ (1 << k)
        first = r < p
        tile = bank_ref[table[jnp.minimum(r, p) * table_width + k + 1]]
        return jnp.where(first, tile, tile.T)

    def own_tile(table, r):
        tile = bank_ref[table[r * table_width]]
        return 0.5 * (tile + tile.T)

    table_width = 5
    uh[...] = jnp.zeros_like(uh)
    ul[...] = jnp.zeros_like(ul)
    dh[...] = jnp.zeros_like(dh)
    dl[...] = jnp.zeros_like(dl)
    for ref in (urh, url, drh, drl):
        ref[...] = jnp.zeros_like(ref)

    def put(refs, index, value):
        high, lo = split(value)
        refs[0][index] = high
        refs[1][index] = lo

    def window(i):
        return slice(i * 128, (i + 1) * 128)

    for i in range(4):
        r = (i // 2) * 8 + low * 4 + y * 2 + i % 2
        put((uh, ul), (window(i), window(i)), own_tile(uidx_ref, r))
        put((uh, ul), (window(i), window(i ^ 1)), pair(uidx_ref, r, 0))
        put((uh, ul), (window(i), window(i ^ 2)), pair(uidx_ref, r, 3))
        for d in range(2):
            put((urh, url), (d, i // 2, window(i % 2), window(i % 2)), pair(uidx_ref, r, 1 + d))
        q = core * 8 + x * 4 + i
        put((dh, dl), (window(i), window(i)), own_tile(didx_ref, q))
        put((dh, dl), (window(i), window(i ^ 1)), pair(didx_ref, q, 0))
        put((dh, dl), (window(i), window(i ^ 2)), pair(didx_ref, q, 1))
        for d in range(2):
            put((drh, drl), (d, i // 2, window(i % 2), window(i % 2)), pair(didx_ref, q, 3 - d).T)

    for copy in side_copies:
        copy.wait()
    mine, other = pay_ref[0:16, :], side[0, 0:16, :]
    ups = jnp.concatenate(
        [jnp.where(h == 0, mine, other), jnp.where(h == 0, other, mine)], axis=1
    )
    energy = jnp.where(on_diagonal, pay_ref[16:32, :], side[1, 16:32, :])
    energy = jnp.concatenate([energy, energy], axis=1)
    dns = dn_ref[:, pl.ds(pl.multiple_of(x * HALF, HALF), HALF)]
    pot[...] = (
        lax.dot_general(
            ups, dns + energy, (((0,), (0,)), ((), ())),
            precision=highest, preferred_element_type=jnp.float32,
        )
        + jnp.sum(energy * dns, axis=0, keepdims=True)
        - 3.5
    )

    finish(regroup(0))
    start(regroup(1))
    for d in range(4):
        exchange(0, d).start()

    def local(t):
        for rb in range(2):
            rows = slice(rb * 256, rb * 256 + 256)
            high, lo = split(field[t, rows, :])
            xh[rows, :] = high
            xl[rows, :] = lo
        for rb in range(2):
            rows = slice(rb * 256, rb * 256 + 256)
            for cb in range(2):
                cols = slice(cb * 256, cb * 256 + 256)
                field[t + 3, rows, cols] = (
                    pot[rows, cols] * field[t, rows, cols]
                    + product((uh[rows, :], ul[rows, :]), (xh[:, cols], xl[:, cols]))
                    + product((xh[rows, :], xl[rows, :]), (dh[:, cols], dl[:, cols]))
                )

    def from_dn(t, d):
        for cb in range(2):
            cols = slice(cb * 256, cb * 256 + 256)
            for rb in range(2):
                rows = slice(rb * 256, rb * 256 + 256)
                field[t + 3, rows, cols] += product(
                    split(got[t, d, rows, cols]), (drh[d, cb], drl[d, cb])
                )

    def from_up(t, d):
        for rb in range(2):
            rows = slice(rb * 256, rb * 256 + 256)
            for cb in range(2):
                cols = slice(cb * 256, cb * 256 + 256)
                field[t + 3, rows, cols] += product(
                    (urh[d - 2, rb], url[d - 2, rb]), split(got[t, d, rows, cols])
                )

    def step(t, carry):
        @pl.when(t < 2)
        def _():
            finish(regroup(t + 1))

            @pl.when(t < 1)
            def _():
                start(regroup(t + 2))

            for d in range(4):
                exchange(t + 1, d).start()

        local(t)
        for d in range(4):
            exchange(t, d).wait()
            (from_dn if d < 2 else from_up)(t, d)

        @pl.when(t < 3)
        def _():
            for d in range(4):
                exchange(t + 3, d).start()

        @pl.when(t >= 3)
        def _():
            start(restore(t - 3))

        return carry

    lax.fori_loop(0, 6, step, 0)

    def chunk(i, sums):
        rows = pl.ds(pl.multiple_of(i * 16, 16), 16)
        firsts = [field[3 + v, rows, :] for v in range(3)]
        seconds = [field[6 + v, rows, :] for v in range(3)]
        terms = [firsts[v] * firsts[w] for v, w in PAIRS]
        terms += [firsts[v] * seconds[w] for v in range(3) for w in range(3)]
        return [s + (term[0:8] + term[8:16]) for s, term in zip(sums, terms)]

    sums = lax.fori_loop(0, HALF // 16, chunk, [jnp.zeros((8, HALF), jnp.float32)] * 15)
    for i in range(15):
        stat_ref[i : i + 1, :] = jnp.sum(sums[i], axis=0, keepdims=True)
    stat_ref[15:16, :] = jnp.zeros((1, HALF), jnp.float32)
    for v in range(3):
        finish(restore(v))


def fused(start, up_occupied, dn_occupied, disorder, hop_tiles, up_index, dn_index):
    sites = up_occupied.shape[1]
    up_part = jnp.pad(up_occupied.astype(jnp.float32).T, ((0, 16 - sites), (0, 0)))
    dn_part = jnp.pad(dn_occupied.astype(jnp.float32).T, ((0, 16 - sites), (0, 0)))
    energies = jnp.broadcast_to(jnp.pad(disorder, (0, 16 - sites))[:, None], (16, ROWS))
    payload = jnp.concatenate([up_part, energies], axis=0)
    vmem = pl.BlockSpec(memory_space=pltpu.VMEM)
    smem = pl.BlockSpec(memory_space=pltpu.SMEM)
    whole = pl.BlockSpec(memory_space=pl.ANY)
    f32, b16, dma = jnp.float32, jnp.bfloat16, pltpu.SemaphoreType.DMA
    second, stats = pl.pallas_call(
        kernel,
        out_shape=[
            jax.ShapeDtypeStruct(start.shape, f32),
            jax.ShapeDtypeStruct((16, HALF), f32),
        ],
        in_specs=[whole, vmem, vmem, vmem, smem, smem],
        out_specs=[whole, vmem],
        scratch_shapes=[
            pltpu.VMEM((9, HALF, HALF), f32),
            pltpu.VMEM((6, 4, HALF, HALF), f32),
            pltpu.VMEM((2, 32, ROWS), f32),
            pltpu.VMEM((HALF, HALF), f32),
        ]
        + [pltpu.VMEM((HALF, HALF), b16)] * 6
        + [pltpu.VMEM((2, 2, 256, 256), b16)] * 4
        + [dma((3, 2)), dma((3, 2)), dma((6, 4)), dma((6, 4)), dma((3, 2)), dma((3, 2)), dma((2,)), dma((2,))],
        compiler_params=pltpu.CompilerParams(
            collective_id=0, has_side_effects=True, vmem_limit_bytes=56 * 1024 * 1024
        ),
    )(start, payload, dn_part, hop_tiles, up_index.reshape(-1), dn_index.reshape(-1))
    cells = start.shape[1] * start.shape[2] * lax.axis_size("up") * lax.axis_size("dn")
    group = lax.axis_index("up") // 4
    sums = jnp.sum(stats, axis=1)
    sums = jnp.where(jnp.arange(2)[:, None] == group, sums[None, :], 0.0)
    sums = lax.psum(sums, ("real", "up", "dn"))
    sums = jnp.where(lax.axis_index("real") == 0, sums[0], sums[1])
    correlation = sums[np.array([0, 1, 2, 1, 3, 4, 2, 4, 5])].reshape(3, 3)
    image = sums[6:15].reshape(3, 3)
    scale = jnp.sqrt(jnp.diagonal(correlation) / cells + 1e-06)
    outer = scale[:, None] * scale[None, :]
    gram = jnp.stack([correlation / outer, image / outer]) / cells
    return (second / scale[:, None, None], gram)


def route(start, *rest):
    sizes = [lax.axis_size(axis) for axis in ("real", "up", "dn")]
    fits = start.shape == (3, 256, 1024) and rest[3].shape == (16, 128, 128)
    if sizes == [2, 8, 2] and fits and rest[0].shape[1] == 14:
        return fused(start, *rest)
    return body(start, *rest)


def solution(mesh):
    return jax.shard_map(
        route,
        mesh=mesh,
        in_specs=(P("real", "up", "dn"), P("up", None), P("dn", None), P("real"), P(), P(), P()),
        out_specs=(P("real", "up", "dn"), P("real", None, None)),
        check_vma=False,
    )
```

```python
import jax
import jax.numpy as jnp
import numpy as np
from jax import lax
from jax.experimental import pallas as pl
from jax.experimental.pallas import tpu as pltpu
from jax.sharding import PartitionSpec as P

highest = lax.Precision.HIGHEST


def swapped(block, axis, bit):
    count = lax.axis_size(axis)
    route = []
    for low in range(count):
        high = low | 1 << bit
        if high != low and high < count:
            route += [(low, high), (high, low)]
    return lax.ppermute(block, axis, route)


def pair_tiles(bank, table, rows, bit):
    others = rows ^ 1 << bit
    lower = jnp.minimum(rows, others)
    picked = bank[table[lower, bit + 1]]
    flipped = jnp.swapaxes(picked, 1, 2)
    return jnp.where((rows < others)[:, None, None], picked, flipped)


def own_tiles(bank, table, rows):
    picked = bank[table[rows, 0]]
    return 0.5 * (picked + jnp.swapaxes(picked, 1, 2))


def row_terms(blocks, rows, bank, table):
    total = jnp.einsum("jab,vjbc->vjac", own_tiles(bank, table, rows), blocks, precision=highest)
    partner = np.arange(blocks.shape[1]) ^ 1 << 0
    total = total + jnp.einsum(
        "jab,vjbc->vjac", pair_tiles(bank, table, rows, 0), blocks[:, partner], precision=highest
    )
    return total


def column_terms(blocks, rows, bank, table, local_bits):
    total = jnp.einsum("jab,vujb->vuja", own_tiles(bank, table, rows), blocks, precision=highest)
    for bit in range(local_bits):
        partner = np.arange(blocks.shape[2]) ^ 1 << bit
        total = total + jnp.einsum(
            "jab,vujb->vuja",
            pair_tiles(bank, table, rows, bit),
            blocks[:, :, partner],
            precision=highest,
        )
    return total


def up_swapped(field, bank, table):
    width = bank.shape[1]
    local = field.shape[1] // width
    local_bits = local.bit_length() - 1
    rows = lax.axis_index("up") * local + jnp.arange(local, dtype=jnp.int32)
    shape = (field.shape[0], local, width, field.shape[2])
    total = row_terms(field.reshape(shape), rows, bank, table)
    for level in range(lax.axis_size("up").bit_length() - 1):
        other = swapped(field, "up", level)
        tiles = pair_tiles(bank, table, rows, local_bits + level)
        total = total + jnp.einsum("jab,vjbc->vjac", tiles, other.reshape(shape), precision=highest)
    return total.reshape(field.shape)


def dn_swapped(field, bank, table):
    width = bank.shape[1]
    local = field.shape[2] // width
    local_bits = local.bit_length() - 1
    rows = lax.axis_index("dn") * local + jnp.arange(local, dtype=jnp.int32)
    shape = (field.shape[0], field.shape[1], local, width)
    total = column_terms(field.reshape(shape), rows, bank, table, local_bits)
    other = swapped(field, "dn", 0)
    tiles = pair_tiles(bank, table, rows, local_bits)
    total = total + jnp.einsum("jab,vujb->vuja", tiles, other.reshape(shape), precision=highest)
    return total.reshape(field.shape)


def operate(field, potential, bank, up_table, dn_table, shift):
    up_part = up_swapped(field, bank, up_table)
    dn_part = dn_swapped(field, bank, dn_table)
    return up_part + dn_part + (potential - shift)[None] * field


def body(start, up_occupied, dn_occupied, disorder, hop_tiles, up_index, dn_index):
    up_float = up_occupied.astype(jnp.float32)
    dn_float = dn_occupied.astype(jnp.float32)
    potential = jnp.dot(up_float, dn_float.T, precision=highest)
    potential = potential + jnp.dot(up_float, disorder, precision=highest)[:, None]
    potential = potential + jnp.dot(dn_float, disorder, precision=highest)[None, :]
    shift = 0.25 * up_occupied.shape[1]
    cells = start.shape[1] * start.shape[2] * lax.axis_size("up") * lax.axis_size("dn")
    first = operate(start, potential, hop_tiles, up_index, dn_index, shift)
    second = operate(first, potential, hop_tiles, up_index, dn_index, shift)
    correlation, image = lax.psum(
        (
            jnp.einsum("vud,wud->vw", first, first, precision=highest),
            jnp.einsum("vud,wud->vw", first, second, precision=highest),
        ),
        ("up", "dn"),
    )
    scale = jnp.sqrt(jnp.diagonal(correlation) / cells + 1e-06)
    outer = scale[:, None] * scale[None, :]
    gram = jnp.stack([correlation / outer, image / outer]) / cells
    return (second / scale[:, None, None], gram)


MESH = pl.DeviceIdType.MESH
HALF = 512
ROWS = 256
PARTS = 2
PART = ROWS // PARTS
PAIRS = [(0, 0), (0, 1), (0, 2), (1, 1), (1, 2), (2, 2)]


def split(value):
    high = value.astype(jnp.bfloat16)
    return high, (value - high.astype(jnp.float32)).astype(jnp.bfloat16)


def product(a, b):
    def dot(p, q):
        return jnp.dot(p, q, preferred_element_type=jnp.float32)

    return dot(a[0], b[0]) + (dot(a[1], b[0]) + dot(a[0], b[1]))


def kernel(
    x_ref, pay_ref, dn_ref, bank_ref, uidx_ref, didx_ref,
    out_ref, stat_ref,
    field, got, side, pot, xh, xl, uh, ul, dh, dl, urh, url, drh, drl,
    hop, rsend, rrecv, rown, hrecv, osend, orecv, bsend, brecv, bown, psend, precv, given, taken, gsend, grecv,
):
    x, up, core = lax.axis_index("real"), lax.axis_index("up"), lax.axis_index("dn")
    z, y = up // 2, up % 2
    h, low = z // 2, z % 2

    def device(px, ph, plow=low, py=y, pc=core):
        return (px, (ph * 2 + plow) * 2 + py, pc)

    partners = [
        device(x, h, pc=1 - core),
        device(1 - x, h),
        device(x, h, py=1 - y),
        device(x, h, plow=1 - low),
    ]
    beside, across = device(1 - x, h), device(x, 1 - h)
    barrier = pltpu.get_barrier_semaphore()
    for partner in partners + [across]:
        pl.semaphore_signal(barrier, inc=1, device_id=partner, device_id_type=MESH)
    pl.semaphore_wait(barrier, 5)

    def remote(src, dst, send, recv, target):
        return pltpu.make_async_remote_copy(
            src_ref=src, dst_ref=dst, send_sem=send, recv_sem=recv,
            device_id=target, device_id_type=MESH,
        )

    on_diagonal = x == h

    def part(c):
        return slice(c * PART, (c + 1) * PART)

    def to_half(i):
        return pl.ds(pl.multiple_of(i * HALF, HALF), HALF)

    def to_rows(i, c=0, count=ROWS):
        return pl.ds(pl.multiple_of(i * ROWS + c * PART, PART), count)

    class Regroup:
        def __init__(self, v):
            near = x_ref.at[v, :, to_half(h)]
            self.own = lambda: pltpu.make_async_copy(
                near, field.at[v, to_rows(h), :], rown.at[v]
            )
            self.far = lambda: remote(
                x_ref.at[v, :, to_half(1 - h)], field.at[v, to_rows(h), :],
                rsend.at[v, PARTS], rrecv.at[v, PARTS], device(1 - h, x),
            )
            self.hops = lambda: [
                remote(
                    x_ref.at[v, part(c), to_half(h)], hop.at[v, part(c), :],
                    rsend.at[v, c], hrecv.at[v, c], beside,
                )
                for c in range(PARTS)
            ]
            self.relays = lambda: [
                remote(
                    hop.at[v, part(c), :], field.at[v, to_rows(h, c, PART), :],
                    rsend.at[v, c], rrecv.at[v, c], across,
                )
                for c in range(PARTS)
            ]

    class Restore:
        def __init__(self, v):
            self.own = lambda: pltpu.make_async_copy(
                field.at[6 + v, to_rows(x), :], out_ref.at[v, :, to_half(x)], bown.at[v]
            )
            self.far = lambda: remote(
                field.at[6 + v, to_rows(1 - x), :], out_ref.at[v, :, to_half(x)],
                bsend.at[v, PARTS], brecv.at[v, PARTS], device(h, 1 - x),
            )
            self.hops = lambda: [
                remote(
                    field.at[6 + v, to_rows(x, c, PART), :], hop.at[3 + v, part(c), :],
                    bsend.at[v, c], hrecv.at[3 + v, c], across,
                )
                for c in range(PARTS)
            ]
            self.relays = lambda: [
                remote(
                    hop.at[3 + v, part(c), :], out_ref.at[v, part(c), to_half(x)],
                    bsend.at[v, c], brecv.at[v, c], beside,
                )
                for c in range(PARTS)
            ]

    def launch(move):
        @pl.when(on_diagonal)
        def _():
            move.own().start()

        @pl.when(jnp.logical_not(on_diagonal))
        def _():
            for copy in move.hops():
                copy.start()

        move.far().start()

    def relay(move):
        @pl.when(on_diagonal)
        def _():
            for first, second in zip(move.hops(), move.relays()):
                first.wait_recv()
                second.start()

    def arrive(move):
        @pl.when(on_diagonal)
        def _():
            move.own().wait()

        @pl.when(jnp.logical_not(on_diagonal))
        def _():
            for copy in move.relays():
                copy.wait_recv()

        move.far().wait_recv()

    def drain(move):
        @pl.when(on_diagonal)
        def _():
            for copy in move.relays():
                copy.wait_send()

        @pl.when(jnp.logical_not(on_diagonal))
        def _():
            for copy in move.hops():
                copy.wait_send()

    def exchange(t, d):
        return remote(field.at[t], got.at[t, d], osend.at[t, d], orecv.at[t, d], partners[d])

    side_copies = [
        remote(pay_ref, side.at[0], psend.at[0], precv.at[0], device(x, 1 - h)),
        remote(pay_ref, side.at[1], psend.at[1], precv.at[1], device(1 - x, h)),
    ]
    launch(Regroup(0))
    for copy in side_copies:
        copy.start()


    def pair(table, r, k):
        p = r ^ (1 << k)
        first = r < p
        tile = bank_ref[table[jnp.minimum(r, p) * table_width + k + 1]]
        return jnp.where(first, tile, tile.T)

    def own_tile(table, r):
        tile = bank_ref[table[r * table_width]]
        return 0.5 * (tile + tile.T)

    table_width = 5
    uh[...] = jnp.zeros_like(uh)
    ul[...] = jnp.zeros_like(ul)
    dh[...] = jnp.zeros_like(dh)
    dl[...] = jnp.zeros_like(dl)
    for ref in (urh, url, drh, drl):
        ref[...] = jnp.zeros_like(ref)

    def put(refs, index, value):
        high, lo = split(value)
        refs[0][index] = high
        refs[1][index] = lo

    def window(i):
        return slice(i * 128, (i + 1) * 128)

    for i in range(4):
        r = (i // 2) * 8 + low * 4 + y * 2 + i % 2
        put((uh, ul), (window(i), window(i)), own_tile(uidx_ref, r))
        put((uh, ul), (window(i), window(i ^ 1)), pair(uidx_ref, r, 0))
        put((uh, ul), (window(i), window(i ^ 2)), pair(uidx_ref, r, 3))
        for d in range(2):
            put((urh, url), (d, i // 2, window(i % 2), window(i % 2)), pair(uidx_ref, r, 1 + d))
        q = core * 8 + x * 4 + i
        put((dh, dl), (window(i), window(i)), own_tile(didx_ref, q))
        put((dh, dl), (window(i), window(i ^ 1)), pair(didx_ref, q, 0))
        put((dh, dl), (window(i), window(i ^ 2)), pair(didx_ref, q, 1))
        for d in range(2):
            put((drh, drl), (d, i // 2, window(i % 2), window(i % 2)), pair(didx_ref, q, 3 - d).T)

    for copy in side_copies:
        copy.wait()
    mine, other = pay_ref[0:16, :], side[0, 0:16, :]
    ups = jnp.concatenate(
        [jnp.where(h == 0, mine, other), jnp.where(h == 0, other, mine)], axis=1
    )
    energy = jnp.where(on_diagonal, pay_ref[16:32, :], side[1, 16:32, :])
    energy = jnp.concatenate([energy, energy], axis=1)
    dns = dn_ref[:, pl.ds(pl.multiple_of(x * HALF, HALF), HALF)]
    pot[...] = (
        lax.dot_general(
            ups, dns + energy, (((0,), (0,)), ((), ())),
            precision=highest, preferred_element_type=jnp.float32,
        )
        + jnp.sum(energy * dns, axis=0, keepdims=True)
        - 3.5
    )

    relay(Regroup(0))
    Regroup(0).far().wait_send()
    launch(Regroup(1))
    arrive(Regroup(0))
    for d in range(4):
        exchange(0, d).start()

    def local(t):
        for rb in range(2):
            rows = slice(rb * 256, rb * 256 + 256)
            high, lo = split(field[t, rows, :])
            xh[rows, :] = high
            xl[rows, :] = lo
        for rb in range(2):
            rows = slice(rb * 256, rb * 256 + 256)
            for cb in range(2):
                cols = slice(cb * 256, cb * 256 + 256)
                field[t + 3, rows, cols] = (
                    pot[rows, cols] * field[t, rows, cols]
                    + product((uh[rows, :], ul[rows, :]), (xh[:, cols], xl[:, cols]))
                    + product((xh[rows, :], xl[rows, :]), (dh[:, cols], dl[:, cols]))
                )

    def from_dn(t, d):
        for cb in range(2):
            cols = slice(cb * 256, cb * 256 + 256)
            for rb in range(2):
                rows = slice(rb * 256, rb * 256 + 256)
                field[t + 3, rows, cols] += product(
                    split(got[t, d, rows, cols]), (drh[d, cb], drl[d, cb])
                )

    def from_up(t, d):
        for rb in range(2):
            rows = slice(rb * 256, rb * 256 + 256)
            for cb in range(2):
                cols = slice(cb * 256, cb * 256 + 256)
                field[t + 3, rows, cols] += product(
                    (urh[d - 2, rb], url[d - 2, rb]), split(got[t, d, rows, cols])
                )

    def step(t, carry):
        @pl.when(t < 2)
        def _():
            relay(Regroup(t + 1))
            Regroup(t + 1).far().wait_send()

            @pl.when(t < 1)
            def _():
                launch(Regroup(t + 2))

            arrive(Regroup(t + 1))
            for d in range(4):
                exchange(t + 1, d).start()

        local(t)

        @pl.when(t >= 4)
        def _():
            relay(Restore(t - 4))

        for d in range(4):
            exchange(t, d).wait()
            (from_dn if d < 2 else from_up)(t, d)

        @pl.when(t < 3)
        def _():
            for d in range(4):
                exchange(t + 3, d).start()

        @pl.when(t >= 3)
        def _():
            launch(Restore(t - 3))

        return carry

    lax.fori_loop(0, 6, step, 0)

    def chunk(i, sums):
        rows = pl.ds(pl.multiple_of(i * 16, 16), 16)
        firsts = [field[3 + v, rows, :] for v in range(3)]
        seconds = [field[6 + v, rows, :] for v in range(3)]
        terms = [firsts[v] * firsts[w] for v, w in PAIRS]
        terms += [firsts[v] * seconds[w] for v in range(3) for w in range(3)]
        return [s + (term[0:8] + term[8:16]) for s, term in zip(sums, terms)]

    sums = lax.fori_loop(0, HALF // 16, chunk, [jnp.zeros((8, HALF), jnp.float32)] * 15)
    for i in range(15):
        line = jnp.sum(sums[i], axis=0, keepdims=True)
        line = (line[:, 0:128] + line[:, 128:256]) + (line[:, 256:384] + line[:, 384:512])
        given[0, i : i + 1, :] = line
    given[0, 15:16, :] = jnp.zeros((1, 128), jnp.float32)

    def add(k, target):
        copy = remote(given.at[k], taken.at[k], gsend.at[k], grecv.at[k], target)
        copy.start()
        copy.wait()

    for k in range(4):
        add(k, partners[k])
        given[k + 1] = given[k] + taken[k]
        if k == 0:
            relay(Restore(2))
    add(4, across)
    stat_ref[...] = jnp.where(on_diagonal, given[4], taken[4])
    for v in range(3):
        arrive(Restore(v))
        drain(Restore(v))
        Restore(v).far().wait_send()
        drain(Regroup(v))


def fused(start, up_occupied, dn_occupied, disorder, hop_tiles, up_index, dn_index):
    sites = up_occupied.shape[1]
    up_part = jnp.pad(up_occupied.astype(jnp.float32).T, ((0, 16 - sites), (0, 0)))
    dn_part = jnp.pad(dn_occupied.astype(jnp.float32).T, ((0, 16 - sites), (0, 0)))
    energies = jnp.broadcast_to(jnp.pad(disorder, (0, 16 - sites))[:, None], (16, ROWS))
    payload = jnp.concatenate([up_part, energies], axis=0)
    vmem = pl.BlockSpec(memory_space=pltpu.VMEM)
    smem = pl.BlockSpec(memory_space=pltpu.SMEM)
    whole = pl.BlockSpec(memory_space=pl.ANY)
    f32, b16, dma = jnp.float32, jnp.bfloat16, pltpu.SemaphoreType.DMA
    second, stats = pl.pallas_call(
        kernel,
        out_shape=[
            jax.ShapeDtypeStruct(start.shape, f32),
            jax.ShapeDtypeStruct((16, 128), f32),
        ],
        in_specs=[whole, vmem, vmem, vmem, smem, smem],
        out_specs=[whole, vmem],
        scratch_shapes=[
            pltpu.VMEM((9, HALF, HALF), f32),
            pltpu.VMEM((6, 4, HALF, HALF), f32),
            pltpu.VMEM((2, 32, ROWS), f32),
            pltpu.VMEM((HALF, HALF), f32),
        ]
        + [pltpu.VMEM((HALF, HALF), b16)] * 6
        + [pltpu.VMEM((2, 2, 256, 256), b16)] * 4
        + [pltpu.VMEM((6, ROWS, HALF), f32)]
        + [dma((3, PARTS + 1)), dma((3, PARTS + 1)), dma((3,)), dma((6, PARTS))]
        + [dma((6, 4)), dma((6, 4))]
        + [dma((3, PARTS + 1)), dma((3, PARTS + 1)), dma((3,)), dma((2,)), dma((2,))]
        + [pltpu.VMEM((5, 16, 128), f32), pltpu.VMEM((5, 16, 128), f32), dma((5,)), dma((5,))],
        compiler_params=pltpu.CompilerParams(
            collective_id=0, has_side_effects=True, vmem_limit_bytes=56 * 1024 * 1024
        ),
    )(start, payload, dn_part, hop_tiles, up_index.reshape(-1), dn_index.reshape(-1))
    cells = start.shape[1] * start.shape[2] * lax.axis_size("up") * lax.axis_size("dn")
    sums = jnp.sum(stats, axis=1)
    correlation = sums[np.array([0, 1, 2, 1, 3, 4, 2, 4, 5])].reshape(3, 3)
    image = sums[6:15].reshape(3, 3)
    scale = jnp.sqrt(jnp.diagonal(correlation) / cells + 1e-06)
    outer = scale[:, None] * scale[None, :]
    gram = jnp.stack([correlation / outer, image / outer]) / cells
    return (second / scale[:, None, None], gram)


def route(start, *rest):
    sizes = [lax.axis_size(axis) for axis in ("real", "up", "dn")]
    fits = start.shape == (3, 256, 1024) and rest[3].shape == (16, 128, 128)
    if sizes == [2, 8, 2] and fits and rest[0].shape[1] == 14:
        return fused(start, *rest)
    return body(start, *rest)


def solution(mesh):
    return jax.shard_map(
        route,
        mesh=mesh,
        in_specs=(P("real", "up", "dn"), P("up", None), P("dn", None), P("real"), P(), P(), P()),
        out_specs=(P("real", "up", "dn"), P("real", None, None)),
        check_vma=False,
    )
```
